128 devices in a mesh: replica: 4 (over z), fsdp: 32 (over y, x, core).
Axes of the slice: x: 4, y: 4, z: 4, core: 2. Of those that a mesh axis runs over, the one named last changes fastest.
Arguments:
- anchor: float32 [1024, 8192], P('fsdp'), may hold values from -6 to 6
- momentum: float32 [1024, 8192], P('fsdp'), may hold values from -3 to 3
- local_weights: bfloat16 [4, 1024, 8192], P('replica', 'fsdp'), may hold values from -64 to 64
- tokens: bfloat16 [4, 32768, 8192], P('replica', 'fsdp'), may hold values from -0.06591797 to 0.06591797
Outputs:
- new_anchor: float32 [1024, 8192], P('fsdp')
- new_momentum: float32 [1024, 8192], P('fsdp')
- merged_weights: bfloat16 [4, 1024, 8192], P('replica', 'fsdp')
- gate_out: bfloat16 [4, 32768, 1024], P('replica', 'fsdp')
The draws below stay inside these ranges and needn't reach their ends.
All inputs are finite; a program needn't handle non-finite values.
Results may differ from the reference program's by a relative error of at most 0.015.
Values may be sent and summed in bfloat16 or wider, within the bound.
No kernel may reach another device: no remote copies, remote signals or barrier semaphores. Data moves between devices by JAX's collectives and lax.ppermute only.
A program may use at most 128 MiB of HBM per device.

```python
import math
import jax
import jax.numpy as jnp
from jax import lax

D = 8192
BLOCK = 128
REPLICAS = 4
UNITS = 1024
TOKENS = 32768


def draw_local_weights(key, part):
    key = jax.random.fold_in(key, 11)
    key_rows, key_cols, key_main = jax.random.split(key, 3)
    shape = (REPLICAS, UNITS, D)
    row_scale = jnp.exp(jax.random.uniform(key_rows, (REPLICAS, UNITS, 1), jnp.float32, math.log(0.4), math.log(4.0)))
    col_scale = jnp.exp(jax.random.uniform(key_cols, (1, 1, D), jnp.float32, math.log(0.4), math.log(4.0)))
    values = jnp.clip(jax.random.normal(key_main, shape, jnp.float32), -4.0, 4.0)
    return (values * row_scale * col_scale).astype(jnp.bfloat16)


def levels(own_key, shape, pieces, low, largest):
    def one(dim, blocks):
        heights = jax.random.uniform(jax.random.fold_in(jax.random.fold_in(own_key, 6), dim), (blocks,), jnp.float32, low / len(pieces), largest / len(pieces))
        return jnp.repeat(jnp.exp(heights), shape[dim] // blocks).reshape((-1,) + (1,) * (len(shape) - dim - 1))

    level = one(*pieces[0])
    for cut in pieces[1:]:
        level = level * one(*cut)
    return level


def noise(own_key, shape, scale, reach, pieces=(), held_as=jnp.bfloat16):
    gain = levels(own_key, shape, pieces, -0.22, 0.18) if pieces else 1.0
    values = jax.random.normal(own_key, shape, jnp.float32) * scale * gain
    return jnp.minimum(jnp.maximum(values, -reach), reach).astype(held_as)


def setup_inputs(seed: int = 0) -> dict:
    key_list = jax.random.split(jax.random.key(seed), 5)
    return {
        "anchor": noise(key_list[0], (UNITS, D), 1.0, 6.0, ((0, 32),), jnp.float32),
        "momentum": noise(key_list[1], (UNITS, D), 0.5, 3.0, ((0, 32),), jnp.float32),
        "local_weights": draw_local_weights(jax.random.fold_in(key_list[4], 71), 0),
        "tokens": noise(key_list[3], (REPLICAS, TOKENS, D), 0.011, 0.06591797, ((0, 4), (1, 32))),
    }


def reference(anchor, momentum, local_weights, tokens):
    delta = anchor[None] - local_weights.astype(jnp.float32)
    blocks = delta.reshape(REPLICAS, UNITS, D // BLOCK, BLOCK)
    block_scale = (2.0 * jnp.sqrt(lax.optimization_barrier(jnp.mean(blocks * blocks, axis=3)) + 1e-06)).astype(jnp.bfloat16)
    wide_scale = block_scale.astype(jnp.float32)[..., None]
    codes = jnp.clip(blocks / wide_scale, -1.0, 1.0).astype(jnp.bfloat16)
    decoded = codes.astype(jnp.float32) * wide_scale
    outer_grad = (lax.optimization_barrier(jnp.sum(decoded, axis=0)) / REPLICAS).reshape(UNITS, D)
    new_momentum = 0.9 * momentum + outer_grad
    new_anchor = anchor - 0.7 * (outer_grad + 0.9 * new_momentum)
    merged_weights = (0.5 * local_weights.astype(jnp.float32) + 0.5 * new_anchor[None]).astype(jnp.bfloat16)
    outputs = []
    for replica in range(REPLICAS):
        product = jnp.dot(tokens[replica], merged_weights[replica].T, preferred_element_type=jnp.float32)
        outputs.append(product.astype(jnp.bfloat16))
    gate_out = jnp.stack(outputs, axis=0)
    return (new_anchor, new_momentum, merged_weights, gate_out)
```

```python
import functools

import jax
import jax.numpy as jnp
from jax import lax
from jax.experimental import pallas as pl
from jax.experimental.pallas import tpu as pltpu
from jax.sharding import PartitionSpec as P

SIDE = 4
BLOCK = 128
CHUNKS = 2
MERGE_COLS = 1024
MIB = 1024 * 1024


def fsdp_index(y, x, core):
    return ((y % SIDE) * SIDE + x % SIDE) * 2 + core


def ring_pairs(step, second):
    pairs = []
    for y in range(SIDE):
        for x in range(SIDE):
            for core in range(2):
                along_x = (core == 0) != second
                target = (y, x + step) if along_x else (y + step, x)
                pairs.append((fsdp_index(y, x, core), fsdp_index(*target, core)))
    return pairs


def to_mate(value):
    return lax.ppermute(value, "core", [(0, 1), (1, 0)])


def to_ring(value, step, second):
    return lax.ppermute(value, ("chip", "core"), ring_pairs(step, second))


def to_replica(value, step):
    return lax.ppermute(value, "replica", [(i, (i + step) % SIDE) for i in range(SIDE)])


def merge_body(replica_ref, anchor, momentum, locals_ref, outer_grad, merged):
    rows, width = anchor.shape
    blocks = width // BLOCK

    def stacked(value):
        return jnp.concatenate([value[:, i * BLOCK : (i + 1) * BLOCK] for i in range(blocks)], axis=0)

    local = locals_ref[...].astype(jnp.float32)
    local = jnp.concatenate([stacked(local[r * rows : (r + 1) * rows]) for r in range(SIDE)], axis=0)
    base = stacked(anchor[...])
    delta = jnp.concatenate([base] * SIDE, axis=0) - local
    square = delta * delta
    high = square.astype(jnp.bfloat16)
    low = (square - high.astype(jnp.float32)).astype(jnp.bfloat16)
    spread = jnp.full((BLOCK, BLOCK), 4.0 / BLOCK, jnp.bfloat16)
    mean = jnp.dot(high, spread, preferred_element_type=jnp.float32)
    mean = mean + jnp.dot(low, spread, preferred_element_type=jnp.float32) + 4e-06
    scale = (mean * lax.rsqrt(mean)).astype(jnp.bfloat16).astype(jnp.float32)
    codes = jnp.clip(delta * pl.reciprocal(scale), -1.0, 1.0).astype(jnp.bfloat16)
    decoded = codes.astype(jnp.float32) * scale
    size = blocks * rows
    parts = [decoded[r * size : (r + 1) * size] for r in range(SIDE)]
    grad = ((parts[0] + parts[2]) + (parts[1] + parts[3])) * 0.25
    speed = 0.9 * stacked(momentum[...]) + grad
    anchored = base - 0.7 * (grad + 0.9 * speed)
    blend = 0.5 * local + 0.5 * jnp.concatenate([anchored] * SIDE, axis=0)
    for i in range(blocks):
        cols = slice(i * BLOCK, (i + 1) * BLOCK)
        outer_grad[:, cols] = grad[i * rows : (i + 1) * rows]
        column = [blend[r * size + i * rows : r * size + (i + 1) * rows] for r in range(SIDE)]
        merged[0, :, cols] = jnp.concatenate(column, axis=0).astype(merged.dtype)


def merge(replica, anchor, momentum, gathered):
    rows, width = anchor.shape
    share = rows // SIDE
    steps = width // MERGE_COLS
    per_half = steps // 2
    own = pl.BlockSpec((share, MERGE_COLS), lambda i, replica_ref: (replica_ref[0], i))
    return pl.pallas_call(
        merge_body,
        grid_spec=pltpu.PrefetchScalarGridSpec(
            num_scalar_prefetch=1,
            grid=(steps,),
            in_specs=[own, own, pl.BlockSpec((rows, MERGE_COLS), lambda i, replica_ref: (0, i))],
            out_specs=[
                pl.BlockSpec((share, MERGE_COLS), lambda i, replica_ref: (0, i)),
                pl.BlockSpec((1, rows, MERGE_COLS), lambda i, replica_ref: (i // per_half, 0, i % per_half)),
            ],
        ),
        out_shape=[
            jax.ShapeDtypeStruct((share, width), jnp.float32),
            jax.ShapeDtypeStruct((2, rows, width // 2), jnp.bfloat16),
        ],
        compiler_params=pltpu.CompilerParams(vmem_limit_bytes=12 * MIB),
        name="merge",
    )(replica, anchor, momentum, gathered)


def update_body(anchor, momentum, local, outer_grad, new_anchor, new_momentum, merged):
    grad = outer_grad[...]
    speed = 0.9 * momentum[...] + grad
    anchored = anchor[...] - 0.7 * (grad + 0.9 * speed)
    new_momentum[...] = speed
    new_anchor[...] = anchored
    merged[...] = (0.5 * local[...].astype(jnp.float32) + 0.5 * anchored).astype(merged.dtype)


def update(anchor, momentum, local, outer_grad):
    rows, width = anchor.shape
    tile = pl.BlockSpec((rows, 2 * MERGE_COLS), lambda i: (0, i))
    wide = jax.ShapeDtypeStruct((rows, width), jnp.float32)
    return pl.pallas_call(
        update_body,
        grid=(width // (2 * MERGE_COLS),),
        in_specs=[tile] * 4,
        out_specs=[tile] * 3,
        out_shape=[wide, wide, jax.ShapeDtypeStruct((rows, width), jnp.bfloat16)],
        compiler_params=pltpu.CompilerParams(vmem_limit_bytes=12 * MIB),
        name="update",
    )(anchor, momentum, local, outer_grad)


def load_body(core_ref, tokens, half, sem):
    width = half.shape[1]
    start = pl.multiple_of(core_ref[0] * width, width)
    copy = pltpu.make_async_copy(tokens.at[:, pl.ds(start, width)], half, sem)
    copy.start()
    copy.wait()


def load_half(core, tokens):
    count, width = tokens.shape
    return pl.pallas_call(
        load_body,
        in_specs=[pl.BlockSpec(memory_space=pltpu.SMEM), pl.BlockSpec(memory_space=pltpu.HBM)],
        out_specs=pl.BlockSpec(memory_space=pltpu.VMEM),
        out_shape=jax.ShapeDtypeStruct((count, width // 2), tokens.dtype),
        scratch_shapes=[pltpu.SemaphoreType.DMA(())],
        compiler_params=pltpu.CompilerParams(vmem_limit_bytes=12 * MIB),
        name="load_half",
    )(core, tokens)


def partial_body(per_block, tokens, *refs):
    weights, out = refs[:-1], refs[-1]
    for block in range(out.shape[0]):
        start, total = 0, None
        for piece in weights[block * per_block : (block + 1) * per_block]:
            term = lax.dot_general(
                tokens[:, start : start + piece.shape[1]],
                piece[...],
                (((1,), (1,)), ((), ())),
                preferred_element_type=jnp.float32,
            )
            total = term if total is None else total + term
            start += piece.shape[1]
        out[block] = total.astype(out.dtype)


def partial_sums(tokens, weights):
    count, half = tokens.shape
    blocks, per_block = len(weights), len(weights[0])
    units = weights[0][0].shape[0]
    return pl.pallas_call(
        functools.partial(partial_body, per_block),
        in_specs=[pl.BlockSpec(memory_space=pltpu.VMEM)] * (1 + blocks * per_block),
        out_specs=pl.BlockSpec(memory_space=pltpu.VMEM),
        out_shape=jax.ShapeDtypeStruct((blocks, count, units), jnp.bfloat16),
        compiler_params=pltpu.CompilerParams(vmem_limit_bytes=20 * MIB),
        cost_estimate=pl.CostEstimate(
            flops=2 * count * units * blocks * half,
            bytes_accessed=2 * (count + units * blocks) * half,
            transcendentals=0,
        ),
        name="partial_sums",
    )(tokens, *[piece for block in weights for piece in block])


COMBINE_ROWS = 128


def combine_body(held, out):
    rows = pl.ds(pl.multiple_of(pl.program_id(0) * COMBINE_ROWS, COMBINE_ROWS), COMBINE_ROWS)
    low = lax.broadcasted_iota(jnp.int32, (COMBINE_ROWS, BLOCK), 1) < BLOCK // 2
    for tile in range(out.shape[1] // BLOCK):
        y, x = tile // 2, 2 * (tile % 2)
        cols = slice((y // 2) * BLOCK, (y // 2 + 1) * BLOCK)
        left = held[1, x, rows, cols].astype(jnp.float32)
        right = held[1, x + 1, rows, cols].astype(jnp.float32)
        if y % 2 == 0:
            right = pltpu.roll(right, BLOCK // 2, 1)
        else:
            left = pltpu.roll(left, BLOCK // 2, 1)
        natural = held[0, y, rows, slice((tile % 2) * BLOCK, (tile % 2 + 1) * BLOCK)].astype(jnp.float32)
        out[:, tile * BLOCK : (tile + 1) * BLOCK] = (natural + jnp.where(low, left, right)).astype(out.dtype)


def combine(held):
    _, _, count, units = held.shape
    return pl.pallas_call(
        combine_body,
        grid=(count // COMBINE_ROWS,),
        in_specs=[pl.BlockSpec(memory_space=pltpu.VMEM)],
        out_specs=pl.BlockSpec((COMBINE_ROWS, units * SIDE), lambda i: (i, 0)),
        out_shape=jax.ShapeDtypeStruct((count, units * SIDE), jnp.bfloat16),
        compiler_params=pltpu.CompilerParams(vmem_limit_bytes=12 * MIB),
        name="combine",
    )(held)


def after(value, *others):
    return lax.optimization_barrier((value, *others))[0]


def on_device(anchor, momentum, local_weights, tokens):
    rows, width = anchor.shape
    half = width // 2
    part = half // CHUNKS
    replica = lax.axis_index("replica")
    core = lax.axis_index("core")
    chip = lax.axis_index("chip")
    x = chip % SIDE
    y = chip // SIDE
    core_array = core.astype(jnp.int32).reshape(1)
    first_base = jnp.where(core == 0, x, y)
    second_base = jnp.where(core == 0, y, x)
    local = local_weights[0]
    batch = tokens[0]

    mate_batch = to_mate(batch)
    gathered = lax.all_to_all(local, "replica", 0, 0, tiled=True)
    outer_part, merged_parts = merge(replica.astype(jnp.int32).reshape(1), anchor, momentum, gathered)
    pair = lax.all_to_all(merged_parts.reshape(2 * rows, half), ("core", "replica"), 0, 0, tiled=True)

    blocks = []
    for c in range(CHUNKS):
        piece = pair[:, c * part : (c + 1) * part]
        block = jnp.zeros((SIDE, 2 * rows, part), jnp.bfloat16)
        pieces = [piece] + [to_ring(piece, step, False) for step in (1, 2, 3)]
        for step, piece in enumerate(pieces):
            block = lax.dynamic_update_slice(block, piece[None], ((first_base - step) % SIDE, 0, 0))
        block = block.reshape(SIDE * 2 * rows, part)
        before = to_ring(block, 1, True)
        following = to_ring(block, SIDE - 1, True)
        low = to_ring(before[:, : part // 2], 1, True)
        high = to_ring(following[:, part // 2 :], SIDE - 1, True)
        blocks.append((block, following, before, low, high))

    own_half = load_half(after(core_array, pair), batch)
    mate_half = load_half(core_array, mate_batch)
    first = [[b[0] for b in blocks]]
    middle = [[b[1] for b in blocks], [b[2] for b in blocks]]
    last = [[piece for b in blocks for piece in b[3:]]]
    held = jnp.zeros((2, SIDE, tokens.shape[1], rows * 2 * SIDE), jnp.bfloat16)
    for weights, steps in ((first, (0,)), (middle, (1, 3)), (last, (2,))):
        got = to_mate(partial_sums(mate_half, weights))
        own = partial_sums(own_half, weights)
        for i, step in enumerate(steps):
            held = lax.dynamic_update_slice(held, own[i][None, None], (core, (second_base + step) % SIDE, 0, 0))
            held = lax.dynamic_update_slice(held, got[i][None, None], (1 - core, (first_base + step) % SIDE, 0, 0))
    gate_out = combine(held)

    outer_part = after(outer_part, blocks[0][0])
    outer_grad = jnp.zeros((rows, width), jnp.float32)
    for step in range(SIDE):
        share = to_replica(outer_part, step) if step else outer_part
        outer_grad = lax.dynamic_update_slice(outer_grad, share, (((replica - step) % SIDE) * share.shape[0], 0))
    new_anchor, new_momentum, merged = update(anchor, momentum, local, outer_grad)
    return (new_anchor, new_momentum, merged[None], gate_out[None])


def solution(mesh):
    split = jax.sharding.Mesh(mesh.devices.reshape(SIDE, SIDE * SIDE, 2), ("replica", "chip", "core"))
    fsdp = ("chip", "core")
    return jax.shard_map(
        on_device,
        mesh=split,
        in_specs=(
            P(fsdp, None),
            P(fsdp, None),
            P("replica", fsdp, None),
            P("replica", fsdp, None),
        ),
        out_specs=(
            P(fsdp, None),
            P(fsdp, None),
            P("replica", fsdp, None),
            P("replica", fsdp, None),
        ),
        check_vma=False,
    )
```

```python
import functools

import jax
import jax.numpy as jnp
from jax import lax
from jax.experimental import pallas as pl
from jax.experimental.pallas import tpu as pltpu
from jax.sharding import PartitionSpec as P

SIDE = 4
BLOCK = 128
CHUNKS = 2
MERGE_COLS = 512
UPDATE_COLS = 2048
MIB = 1024 * 1024


def fsdp_index(y, x, core):
    return ((y % SIDE) * SIDE + x % SIDE) * 2 + core


def ring_pairs(step, second):
    pairs = []
    for y in range(SIDE):
        for x in range(SIDE):
            for core in range(2):
                along_x = (core == 0) != second
                target = (y, x + step) if along_x else (y + step, x)
                pairs.append((fsdp_index(y, x, core), fsdp_index(*target, core)))
    return pairs


def in_hbm(value):
    return pltpu.with_memory_space_constraint(value, pltpu.HBM)


def in_vmem(value):
    return pltpu.with_memory_space_constraint(value, pltpu.VMEM)


def to_mate(value):
    return lax.ppermute(value, "core", [(0, 1), (1, 0)])


def to_ring(value, step, second):
    return lax.ppermute(value, ("chip", "core"), ring_pairs(step, second))


def to_replica(value, step):
    return lax.ppermute(value, "replica", [(i, (i + step) % SIDE) for i in range(SIDE)])


def merge_body(anchor, momentum, gathered, outer_grad, merged):
    rows, width = anchor.shape
    blocks = MERGE_COLS // BLOCK
    size = blocks * rows
    spread = jnp.full((BLOCK, BLOCK), 4.0 / BLOCK, jnp.bfloat16)

    def stacked(value):
        return jnp.concatenate([value[:, i * BLOCK : (i + 1) * BLOCK] for i in range(blocks)], axis=0)

    for start in range(0, width, MERGE_COLS):
        cols = slice(start, start + MERGE_COLS)
        local = gathered[:, cols].astype(jnp.float32)
        local = jnp.concatenate([stacked(local[r * rows : (r + 1) * rows]) for r in range(SIDE)], axis=0)
        base = stacked(anchor[:, cols])
        delta = jnp.concatenate([base] * SIDE, axis=0) - local
        square = delta * delta
        high = square.astype(jnp.bfloat16)
        low = (square - high.astype(jnp.float32)).astype(jnp.bfloat16)
        mean = jnp.dot(high, spread, preferred_element_type=jnp.float32)
        mean = mean + jnp.dot(low, spread, preferred_element_type=jnp.float32) + 4e-06
        scale = (mean * lax.rsqrt(mean)).astype(jnp.bfloat16).astype(jnp.float32)
        codes = jnp.clip(delta * pl.reciprocal(scale), -1.0, 1.0).astype(jnp.bfloat16)
        decoded = codes.astype(jnp.float32) * scale
        parts = [decoded[r * size : (r + 1) * size] for r in range(SIDE)]
        grad = ((parts[0] + parts[2]) + (parts[1] + parts[3])) * 0.25
        speed = 0.9 * stacked(momentum[:, cols]) + grad
        anchored = base - 0.7 * (grad + 0.9 * speed)
        blend = (0.5 * local + 0.5 * jnp.concatenate([anchored] * SIDE, axis=0)).astype(merged.dtype)
        for i in range(blocks):
            place = slice(start + i * BLOCK, start + (i + 1) * BLOCK)
            outer_grad[:, place] = grad[i * rows : (i + 1) * rows]
            for r in range(SIDE):
                merged[r * rows : (r + 1) * rows, place] = blend[r * size + i * rows : r * size + (i + 1) * rows]


def merge(anchor, momentum, gathered):
    vmem = pl.BlockSpec(memory_space=pltpu.VMEM)
    return pl.pallas_call(
        merge_body,
        in_specs=[vmem] * 3,
        out_specs=[vmem] * 2,
        out_shape=[
            jax.ShapeDtypeStruct(anchor.shape, jnp.float32),
            jax.ShapeDtypeStruct(gathered.shape, jnp.bfloat16),
        ],
        compiler_params=pltpu.CompilerParams(vmem_limit_bytes=8 * MIB),
        name="merge",
    )(in_vmem(anchor), in_vmem(momentum), in_vmem(gathered))


def update_body(anchor, momentum, local, outer_grad, new_anchor, new_momentum, merged):
    grad = outer_grad[...]
    speed = 0.9 * momentum[...] + grad
    anchored = anchor[...] - 0.7 * (grad + 0.9 * speed)
    new_momentum[...] = speed
    new_anchor[...] = anchored
    merged[...] = (0.5 * local[...].astype(jnp.float32) + 0.5 * anchored).astype(merged.dtype)


def update(anchor, momentum, local, outer_grad):
    rows, width = anchor.shape
    tile = pl.BlockSpec((rows, UPDATE_COLS), lambda i: (0, i))
    wide = jax.ShapeDtypeStruct((rows, width), jnp.float32)
    return pl.pallas_call(
        update_body,
        grid=(width // (UPDATE_COLS),),
        in_specs=[tile] * 4,
        out_specs=[tile] * 3,
        out_shape=[wide, wide, jax.ShapeDtypeStruct((rows, width), jnp.bfloat16)],
        compiler_params=pltpu.CompilerParams(vmem_limit_bytes=12 * MIB),
        name="update",
    )(in_hbm(anchor), in_hbm(momentum), in_hbm(local), outer_grad)


def load_body(start_ref, tokens, *refs):
    half, sem = refs[-2:]
    start = pl.multiple_of(start_ref[0], half.shape[1])
    copy = pltpu.make_async_copy(tokens.at[:, pl.ds(start, half.shape[1])], half, sem)
    copy.start()
    copy.wait()


def load_columns(start, tokens, width, *earlier):
    anywhere = pl.BlockSpec(memory_space=pl.ANY)
    return pl.pallas_call(
        load_body,
        in_specs=[pl.BlockSpec(memory_space=pltpu.SMEM), pl.BlockSpec(memory_space=pltpu.HBM)]
        + [anywhere] * len(earlier),
        out_specs=pl.BlockSpec(memory_space=pltpu.VMEM),
        out_shape=pltpu.VMEM((tokens.shape[0], width), tokens.dtype),
        scratch_shapes=[pltpu.SemaphoreType.DMA(())],
        compiler_params=pltpu.CompilerParams(vmem_limit_bytes=2 * MIB),
        name="load_columns",
    )(start.astype(jnp.int32).reshape(1), in_hbm(tokens), *earlier)


def partial_body(per_block, tokens, *refs):
    weights, out = refs[:-1], refs[-1]
    for block in range(out.shape[0]):
        start, total = 0, None
        for piece in weights[block * per_block : (block + 1) * per_block]:
            term = lax.dot_general(
                tokens[:, start : start + piece.shape[1]],
                piece[...],
                (((1,), (1,)), ((), ())),
                preferred_element_type=jnp.float32,
            )
            total = term if total is None else total + term
            start += piece.shape[1]
        out[block] = total.astype(out.dtype)


def partial_sums(tokens, weights):
    count, half = tokens.shape
    blocks, per_block = len(weights), len(weights[0])
    units = weights[0][0].shape[0]
    vmem = pl.BlockSpec(memory_space=pltpu.VMEM)
    return pl.pallas_call(
        functools.partial(partial_body, per_block),
        in_specs=[vmem] * (1 + blocks * per_block),
        out_specs=vmem,
        out_shape=jax.ShapeDtypeStruct((blocks, count, units), jnp.bfloat16),
        compiler_params=pltpu.CompilerParams(vmem_limit_bytes=16 * MIB),
        cost_estimate=pl.CostEstimate(
            flops=2 * count * units * blocks * half,
            bytes_accessed=2 * (count + units * blocks) * half,
            transcendentals=0,
        ),
        name="partial_sums",
    )(in_vmem(tokens), *[in_vmem(piece) for block in weights for piece in block])


COMBINE_ROWS = 256


def combine_body(held, out):
    rows = pl.ds(pl.multiple_of(pl.program_id(0) * COMBINE_ROWS, COMBINE_ROWS), COMBINE_ROWS)
    low = lax.broadcasted_iota(jnp.int32, (COMBINE_ROWS, BLOCK), 1) < BLOCK // 2
    for x in (0, 2):
        for k in range(SIDE // 2):
            cols = slice(k * BLOCK, (k + 1) * BLOCK)
            left = held[1, x, rows, cols].astype(jnp.float32)
            right = held[1, x + 1, rows, cols].astype(jnp.float32)
            crossed = pltpu.roll(jnp.where(low, right, left), BLOCK // 2, 1)
            for y, term in ((2 * k, jnp.where(low, left, crossed)), (2 * k + 1, jnp.where(low, crossed, right))):
                natural = held[0, y, rows, slice(x // 2 * BLOCK, (x // 2 + 1) * BLOCK)].astype(jnp.float32)
                start = (2 * y + x // 2) * BLOCK
                out[:, start : start + BLOCK] = (natural + term).astype(out.dtype)


def combine(held):
    _, _, count, units = held.shape
    return pl.pallas_call(
        combine_body,
        grid=(count // COMBINE_ROWS,),
        in_specs=[pl.BlockSpec(memory_space=pltpu.VMEM)],
        out_specs=pl.BlockSpec((COMBINE_ROWS, units * SIDE), lambda i: (i, 0)),
        out_shape=jax.ShapeDtypeStruct((count, units * SIDE), jnp.bfloat16),
        compiler_params=pltpu.CompilerParams(vmem_limit_bytes=12 * MIB),
        name="combine",
    )(held)


def on_device(anchor, momentum, local_weights, tokens):
    rows, width = anchor.shape
    half = width // 2
    part = half // CHUNKS
    replica = lax.axis_index("replica")
    core = lax.axis_index("core")
    chip = lax.axis_index("chip")
    x = chip % SIDE
    y = chip // SIDE
    first_base = jnp.where(core == 0, x, y)
    second_base = jnp.where(core == 0, y, x)
    local = local_weights[0]
    batch = tokens[0]

    share = rows // SIDE
    mine, other = core * half, (1 - core) * half
    row = replica * share

    def both_cores(own, got):
        return jnp.where(core == 0, jnp.stack([own, got]), jnp.stack([got, own]))

    def columns(value, start):
        return lax.dynamic_slice(value, (0, start), (value.shape[0], half))

    state = jnp.concatenate(
        [lax.dynamic_slice(value, (row, 0), (share, width)) for value in (anchor, momentum)], axis=0
    )
    local_pair = both_cores(columns(local, mine), to_mate(columns(local, other)))
    state_pair = both_cores(columns(state, mine), to_mate(columns(state, other)))
    local_pair = local_pair.reshape(2, SIDE, share, half).transpose(1, 0, 2, 3)
    own_anchor, own_momentum = state_pair.reshape(2, 2, share, half).transpose(1, 0, 2, 3).reshape(2, 2 * share, half)

    def share_of(value, step):
        return lax.dynamic_slice(value, ((replica + step) % SIDE, 0, 0, 0), (1,) + value.shape[1:])

    def exchange(value):
        pieces = [(step, to_replica(share_of(value, step), step)) for step in (1, 3, 2)]
        return [(0, share_of(value, 0))] + pieces

    gathered = jnp.zeros_like(local_pair)
    received = exchange(local_pair)
    mate_half = to_mate(load_columns(other, batch, half, received[1][1], own_anchor))
    for step, piece in received:
        gathered = lax.dynamic_update_slice(gathered, piece, ((replica - step) % SIDE, 0, 0, 0))
    gathered = gathered.reshape(SIDE * 2 * share, half)
    outer_part, merged_parts = merge(own_anchor, own_momentum, gathered)
    pair = jnp.zeros((2, SIDE, share, half), jnp.bfloat16)
    for step, piece in exchange(merged_parts.reshape(SIDE, 2, share, half)):
        pair = lax.dynamic_update_slice(pair, piece.reshape(2, 1, share, half), (0, (replica - step) % SIDE, 0, 0))
    pair = pair.reshape(2 * rows, half)

    own_half = load_columns(mine, batch, half, pair)
    block = jnp.zeros((SIDE, 2 * rows, half), jnp.bfloat16)
    pieces = [pair] + [to_ring(pair, step, False) for step in (1, 3, 2)]
    for step, piece in zip((0, 1, 3, 2), pieces):
        block = lax.dynamic_update_slice(block, piece[None], ((first_base - step) % SIDE, 0, 0))
    whole = block.reshape(SIDE * 2 * rows, half)
    blocks = []
    for c in range(CHUNKS):
        block = whole[:, c * part : (c + 1) * part]
        before = to_ring(block, 1, True)
        following = to_ring(block, SIDE - 1, True)
        low = to_ring(before[:, : part // 2], 1, True)
        high = to_ring(following[:, part // 2 :], SIDE - 1, True)
        blocks.append((block, following, before, low, high))

    first = [[b[0] for b in blocks]]
    middle = [[b[1] for b in blocks], [b[2] for b in blocks]]
    last = [[piece for b in blocks for piece in b[3:]]]
    held = jnp.zeros((2, SIDE, tokens.shape[1], rows * 2 * SIDE), jnp.bfloat16)

    def place(held, which, base, steps, sums):
        for i, step in enumerate(steps):
            held = lax.dynamic_update_slice(held, sums[i][None, None], (which, (base + step) % SIDE, 0, 0))
        return held

    held = place(held, core, second_base, (0,), partial_sums(own_half, first))
    got = to_mate(partial_sums(mate_half, first + middle))
    held = place(held, core, second_base, (1, 3), partial_sums(own_half, middle))
    held = place(held, 1 - core, first_base, (0, 1, 3), got)
    got = to_mate(partial_sums(mate_half, last))
    held = place(held, core, second_base, (2,), partial_sums(own_half, last))
    held = place(held, 1 - core, first_base, (2,), got)
    gate_out = combine(held)

    grads = jnp.zeros((SIDE, 2, share, half), jnp.float32)
    outer_part = outer_part.reshape(1, 2, share, half)
    grads = lax.dynamic_update_slice(grads, outer_part, (replica, 0, 0, 0))
    neighbour = lax.ppermute(outer_part, "replica", [(i, i ^ 1) for i in range(SIDE)])
    grads = lax.dynamic_update_slice(grads, neighbour, (replica ^ 1, 0, 0, 0))
    both = jnp.concatenate([outer_part, neighbour])
    opposite = lax.ppermute(both, "replica", [(i, i ^ 3) for i in range(SIDE)])
    grads = lax.dynamic_update_slice(grads, opposite[:1], (replica ^ 3, 0, 0, 0))
    grads = lax.dynamic_update_slice(grads, opposite[1:], (replica ^ 2, 0, 0, 0))

    def rows_of(which):
        return lax.dynamic_slice(grads, (0, which, 0, 0), (SIDE, 1, share, half)).reshape(rows, half)

    own_grad, mate_grad = rows_of(core), to_mate(rows_of(1 - core))
    outer_grad = jnp.where(
        core == 0, jnp.concatenate([own_grad, mate_grad], axis=1), jnp.concatenate([mate_grad, own_grad], axis=1)
    )
    new_anchor, new_momentum, merged = update(anchor, momentum, local, outer_grad)
    return (new_anchor, new_momentum, merged[None], gate_out[None])


def solution(mesh):
    split = jax.sharding.Mesh(mesh.devices.reshape(SIDE, SIDE * SIDE, 2), ("replica", "chip", "core"))
    fsdp = ("chip", "core")
    return jax.shard_map(
        on_device,
        mesh=split,
        in_specs=(
            P(fsdp, None),
            P(fsdp, None),
            P("replica", fsdp, None),
            P("replica", fsdp, None),
        ),
        out_specs=(
            P(fsdp, None),
            P(fsdp, None),
            P("replica", fsdp, None),
            P("replica", fsdp, None),
        ),
        check_vma=False,
    )
```

```python
import functools

import jax
import jax.numpy as jnp
from jax import lax
from jax.experimental import pallas as pl
from jax.experimental.pallas import tpu as pltpu
from jax.sharding import PartitionSpec as P

SIDE = 4
BLOCK = 128
CHUNKS = 2
MERGE_COLS = 512
UPDATE_COLS = 2048
CHEAP = pl.CostEstimate(flops=1024, bytes_accessed=1024, transcendentals=0)
MIB = 1024 * 1024


def fsdp_index(y, x, core):
    return ((y % SIDE) * SIDE + x % SIDE) * 2 + core


def ring_pairs(step, second):
    pairs = []
    for y in range(SIDE):
        for x in range(SIDE):
            for core in range(2):
                along_x = (core == 0) != second
                target = (y, x + step) if along_x else (y + step, x)
                pairs.append((fsdp_index(y, x, core), fsdp_index(*target, core)))
    return pairs


def in_hbm(value):
    return pltpu.with_memory_space_constraint(value, pltpu.HBM)


def in_vmem(value):
    return pltpu.with_memory_space_constraint(value, pltpu.VMEM)


def to_mate(value):
    return lax.ppermute(value, "core", [(0, 1), (1, 0)])


def to_ring(value, step, second):
    return lax.ppermute(value, ("chip", "core"), ring_pairs(step, second))


def to_replica(value, step):
    return lax.ppermute(value, "replica", [(i, (i + step) % SIDE) for i in range(SIDE)])


def merge_body(anchor, momentum, gathered, outer_grad, merged):
    rows, width = anchor.shape
    blocks = MERGE_COLS // BLOCK
    size = blocks * rows
    spread = jnp.full((BLOCK, BLOCK), 4.0 / BLOCK, jnp.bfloat16)

    def stacked(value):
        return jnp.concatenate([value[:, i * BLOCK : (i + 1) * BLOCK] for i in range(blocks)], axis=0)

    for start in range(0, width, MERGE_COLS):
        cols = slice(start, start + MERGE_COLS)
        local = gathered[:, cols].astype(jnp.float32)
        local = jnp.concatenate([stacked(local[r * rows : (r + 1) * rows]) for r in range(SIDE)], axis=0)
        base = stacked(anchor[:, cols])
        delta = jnp.concatenate([base] * SIDE, axis=0) - local
        square = delta * delta
        high = square.astype(jnp.bfloat16)
        low = (square - high.astype(jnp.float32)).astype(jnp.bfloat16)
        mean = jnp.dot(high, spread, preferred_element_type=jnp.float32)
        mean = mean + jnp.dot(low, spread, preferred_element_type=jnp.float32) + 4e-06
        scale = (mean * lax.rsqrt(mean)).astype(jnp.bfloat16).astype(jnp.float32)
        codes = jnp.clip(delta * pl.reciprocal(scale), -1.0, 1.0).astype(jnp.bfloat16)
        decoded = codes.astype(jnp.float32) * scale
        parts = [decoded[r * size : (r + 1) * size] for r in range(SIDE)]
        grad = ((parts[0] + parts[2]) + (parts[1] + parts[3])) * 0.25
        speed = 0.9 * stacked(momentum[:, cols]) + grad
        anchored = base - 0.7 * (grad + 0.9 * speed)
        blend = (0.5 * local + 0.5 * jnp.concatenate([anchored] * SIDE, axis=0)).astype(merged.dtype)
        for i in range(blocks):
            place = slice(start + i * BLOCK, start + (i + 1) * BLOCK)
            outer_grad[:, place] = grad[i * rows : (i + 1) * rows]
            for r in range(SIDE):
                merged[r * rows : (r + 1) * rows, place] = blend[r * size + i * rows : r * size + (i + 1) * rows]


def merge(anchor, momentum, gathered):
    vmem = pl.BlockSpec(memory_space=pltpu.VMEM)
    return pl.pallas_call(
        merge_body,
        in_specs=[vmem] * 3,
        out_specs=[vmem] * 2,
        out_shape=[
            jax.ShapeDtypeStruct(anchor.shape, jnp.float32),
            jax.ShapeDtypeStruct(gathered.shape, jnp.bfloat16),
        ],
        compiler_params=pltpu.CompilerParams(vmem_limit_bytes=8 * MIB),
        cost_estimate=CHEAP,
        name="merge",
    )(in_vmem(anchor), in_vmem(momentum), in_vmem(gathered))


def update_body(anchor, momentum, local, outer_grad, new_anchor, new_momentum, merged):
    grad = outer_grad[...]
    speed = 0.9 * momentum[...] + grad
    anchored = anchor[...] - 0.7 * (grad + 0.9 * speed)
    new_momentum[...] = speed
    new_anchor[...] = anchored
    merged[...] = (0.5 * local[...].astype(jnp.float32) + 0.5 * anchored).astype(merged.dtype)


def update(anchor, momentum, local, outer_grad):
    rows, width = anchor.shape
    tile = pl.BlockSpec((rows, UPDATE_COLS), lambda i: (0, i))
    wide = jax.ShapeDtypeStruct((rows, width), jnp.float32)
    return pl.pallas_call(
        update_body,
        grid=(width // (UPDATE_COLS),),
        in_specs=[tile] * 4,
        out_specs=[tile] * 3,
        out_shape=[wide, wide, jax.ShapeDtypeStruct((rows, width), jnp.bfloat16)],
        compiler_params=pltpu.CompilerParams(vmem_limit_bytes=12 * MIB),
        cost_estimate=CHEAP,
        name="update",
    )(in_hbm(anchor), in_hbm(momentum), in_hbm(local), outer_grad)


def load_body(entry, place, tokens, *refs):
    half, sem = refs[-2:]
    start = pl.multiple_of(place[entry], half.shape[1])
    copy = pltpu.make_async_copy(tokens.at[:, pl.ds(start, half.shape[1])], half, sem)
    copy.start()
    copy.wait()


def load_columns(place, entry, tokens, width, *earlier):
    anywhere = pl.BlockSpec(memory_space=pl.ANY)
    return pl.pallas_call(
        functools.partial(load_body, entry),
        in_specs=[pl.BlockSpec(memory_space=pltpu.SMEM), pl.BlockSpec(memory_space=pltpu.HBM)]
        + [anywhere] * len(earlier),
        out_specs=pl.BlockSpec(memory_space=pltpu.VMEM),
        out_shape=pltpu.VMEM((tokens.shape[0], width), tokens.dtype),
        scratch_shapes=[pltpu.SemaphoreType.DMA(())],
        compiler_params=pltpu.CompilerParams(vmem_limit_bytes=9 * MIB),
        cost_estimate=CHEAP,
        name="load_columns",
    )(place, in_hbm(tokens), *earlier)


def partial_body(per_block, first, count, tokens, *refs):
    weights, out = refs[: count * per_block], refs[-1]
    for block in range(count):
        start, total = 0, None
        for piece in weights[block * per_block : (block + 1) * per_block]:
            term = lax.dot_general(
                tokens[:, start : start + piece.shape[1]],
                piece[...],
                (((1,), (1,)), ((), ())),
                preferred_element_type=jnp.float32,
            )
            total = term if total is None else total + term
            start += piece.shape[1]
        out[first + block] = total.astype(out.dtype)


def partial_sums(tokens, weights, size=None, filled=None, earlier=(), cost=CHEAP):
    count, half = tokens.shape
    blocks, per_block = len(weights), len(weights[0])
    units = weights[0][0].shape[0]
    size = size or blocks
    vmem = pl.BlockSpec(memory_space=pltpu.VMEM)
    anywhere = pl.BlockSpec(memory_space=pl.ANY)
    more = list(earlier) if filled is None else [*earlier, filled]
    operands = 1 + blocks * per_block
    return pl.pallas_call(
        functools.partial(partial_body, per_block, 0 if filled is None else size - blocks, blocks),
        in_specs=[vmem] * operands + [anywhere] * len(earlier) + ([] if filled is None else [vmem]),
        out_specs=vmem,
        out_shape=jax.ShapeDtypeStruct((size, count, units), jnp.bfloat16),
        input_output_aliases={} if filled is None else {operands + len(earlier): 0},
        compiler_params=pltpu.CompilerParams(vmem_limit_bytes=12 * MIB),
        cost_estimate=cost,
        name="partial_sums",
    )(in_vmem(tokens), *[in_vmem(piece) for block in weights for piece in block], *more)


COMBINE_ROWS = 256


def combine_body(place, own_first, own_mid, own_last, got_first, got_mid, got_last, out, held):
    core = place[0]
    for side, base, first, mid, last in (
        (core, place[1], own_first, own_mid, own_last),
        (1 - core, place[2], got_first, got_mid, got_last),
    ):
        for step, source in ((0, first[0]), (1, mid[0]), (3, mid[1]), (2, last[0])):
            held[side, lax.rem(base + step, SIDE)] = source
    low = lax.broadcasted_iota(jnp.int32, (COMBINE_ROWS, BLOCK), 1) < BLOCK // 2
    for x in (0, 2):
        for k in range(SIDE // 2):
            cols = slice(k * BLOCK, (k + 1) * BLOCK)
            left = held[1, x, :, cols].astype(jnp.float32)
            right = held[1, x + 1, :, cols].astype(jnp.float32)
            crossed = pltpu.roll(jnp.where(low, right, left), BLOCK // 2, 1)
            for y, term in ((2 * k, jnp.where(low, left, crossed)), (2 * k + 1, jnp.where(low, crossed, right))):
                natural = held[0, y, :, slice(x // 2 * BLOCK, (x // 2 + 1) * BLOCK)].astype(jnp.float32)
                start = (2 * y + x // 2) * BLOCK
                out[:, start : start + BLOCK] = (natural + term).astype(out.dtype)


def combine(place, *sums):
    _, count, units = sums[0].shape
    return pl.pallas_call(
        combine_body,
        grid=(count // COMBINE_ROWS,),
        in_specs=[pl.BlockSpec(memory_space=pltpu.SMEM)] + [pl.BlockSpec((value.shape[0], COMBINE_ROWS, units), lambda i: (0, i, 0)) for value in sums],
        out_specs=pl.BlockSpec((COMBINE_ROWS, units * SIDE), lambda i: (i, 0)),
        out_shape=jax.ShapeDtypeStruct((count, units * SIDE), jnp.bfloat16),
        scratch_shapes=[pltpu.VMEM((2, SIDE, COMBINE_ROWS, units), jnp.bfloat16)],
        compiler_params=pltpu.CompilerParams(vmem_limit_bytes=6 * MIB),
        cost_estimate=CHEAP,
        name="combine",
    )(place, *sums)


def follow_body(*refs):
    pass


def follow(values, *earlier):
    vmem = pl.BlockSpec(memory_space=pltpu.VMEM)
    anywhere = pl.BlockSpec(memory_space=pl.ANY)
    return pl.pallas_call(
        follow_body,
        in_specs=[vmem] * len(values) + [anywhere] * len(earlier),
        out_specs=[vmem] * len(values),
        out_shape=[pltpu.VMEM(value.shape, value.dtype) for value in values],
        input_output_aliases={i: i for i in range(len(values))},
        compiler_params=pltpu.CompilerParams(vmem_limit_bytes=4 * MIB),
        cost_estimate=CHEAP,
        name="follow",
    )(*[in_vmem(value) for value in values], *earlier)


def on_device(anchor, momentum, local_weights, tokens):
    rows, width = anchor.shape
    half = width // 2
    part = half // CHUNKS
    replica = lax.axis_index("replica")
    core = lax.axis_index("core")
    chip = lax.axis_index("chip")
    x = chip % SIDE
    y = chip // SIDE
    first_base = jnp.where(core == 0, x, y)
    second_base = jnp.where(core == 0, y, x)
    local = local_weights[0]
    batch = tokens[0]

    share = rows // SIDE
    mine, other = core * half, (1 - core) * half
    row = replica * share
    place = jnp.stack([core, second_base, first_base, mine, other]).astype(jnp.int32)

    def both_cores(own, got):
        return jnp.where(core == 0, jnp.stack([own, got]), jnp.stack([got, own]))

    def columns(value, start):
        return lax.dynamic_slice(value, (0, start), (value.shape[0], half))

    state = jnp.concatenate(
        [lax.dynamic_slice(value, (row, 0), (share, width)) for value in (anchor, momentum)], axis=0
    )
    local_pair = both_cores(columns(local, mine), to_mate(columns(local, other)))
    state_pair = both_cores(columns(state, mine), to_mate(columns(state, other)))
    local_pair = local_pair.reshape(2, SIDE, share, half).transpose(1, 0, 2, 3)
    own_anchor, own_momentum = state_pair.reshape(2, 2, share, half).transpose(1, 0, 2, 3).reshape(2, 2 * share, half)

    def share_of(value, step):
        return lax.dynamic_slice(value, ((replica + step) % SIDE, 0, 0, 0), (1,) + value.shape[1:])

    def exchange(value):
        pieces = [(step, to_replica(share_of(value, step), step)) for step in (1, 3, 2)]
        return [(0, share_of(value, 0))] + pieces

    gathered = jnp.zeros_like(local_pair)
    received = exchange(local_pair)
    mate_half = to_mate(load_columns(place, 4, batch, half, received[1][1], own_anchor))
    for step, piece in received:
        gathered = lax.dynamic_update_slice(gathered, piece, ((replica - step) % SIDE, 0, 0, 0))
    gathered = gathered.reshape(SIDE * 2 * share, half)
    outer_part, merged_parts = merge(own_anchor, own_momentum, gathered)
    outer_part = outer_part.reshape(2, share, half)
    own_part, mate_part = (lax.dynamic_slice(outer_part, (which, 0, 0), (1, share, half))[0] for which in (core, 1 - core))
    mate_part = to_mate(mate_part)
    outer_part = jnp.where(
        core == 0, jnp.concatenate([own_part, mate_part], axis=1), jnp.concatenate([mate_part, own_part], axis=1)
    )
    pair = jnp.zeros((2, SIDE, share, half), jnp.bfloat16)
    for step, piece in exchange(merged_parts.reshape(SIDE, 2, share, half)):
        pair = lax.dynamic_update_slice(pair, piece.reshape(2, 1, share, half), (0, (replica - step) % SIDE, 0, 0))
    pair = pair.reshape(2 * rows, half)

    own_half = load_columns(place, 3, batch, half, pair)
    block = jnp.zeros((SIDE, 2 * rows, half), jnp.bfloat16)
    pieces = [pair] + [to_ring(pair, step, False) for step in (1, 3, 2)]
    for step, piece in zip((0, 1, 3, 2), pieces):
        block = lax.dynamic_update_slice(block, piece[None], ((first_base - step) % SIDE, 0, 0))
    whole = block.reshape(SIDE * 2 * rows, half)
    blocks = []
    for c in range(CHUNKS):
        block = whole[:, c * part : (c + 1) * part]
        blocks.append((block, to_ring(block, SIDE - 1, True), to_ring(block, 1, True)))

    outer_grad = jnp.zeros((rows, width), jnp.float32)
    outer_grad = lax.dynamic_update_slice(outer_grad, outer_part, (row, 0))
    neighbour = lax.ppermute(outer_part, "replica", [(i, i ^ 1) for i in range(SIDE)])
    outer_grad = lax.dynamic_update_slice(outer_grad, neighbour, ((replica ^ 1) * share, 0))
    both = jnp.concatenate([outer_part, neighbour])
    opposite = lax.ppermute(both, "replica", [(i, i ^ 3) for i in range(SIDE)])
    outer_grad = lax.dynamic_update_slice(outer_grad, opposite[:share], ((replica ^ 3) * share, 0))
    outer_grad = lax.dynamic_update_slice(outer_grad, opposite[share:], ((replica ^ 2) * share, 0))
    new_anchor, new_momentum, merged = update(anchor, momentum, local, outer_grad)
    first = [[b[0] for b in blocks]]
    middle = [[b[1] for b in blocks], [b[2] for b in blocks]]
    sums = [partial_sums(mate_half, first)]
    own_sums = [partial_sums(own_half, first)]
    last = []
    for c, (_, following, before) in enumerate(blocks):
        low, high = before[:, : part // 2], following[:, part // 2 :]
        if c == 0:
            low, high = follow([low, high], own_sums[0], merged)
        last += [to_ring(low, 1, True), to_ring(high, SIDE - 1, True)]
    sums.append(partial_sums(mate_half, middle))
    own_sums.append(partial_sums(own_half, middle))
    sums = follow(sums, last[2], own_sums[1])
    got = [to_mate(value) for value in sums]
    cost = pl.CostEstimate(flops=2 * tokens.shape[1] * 2 * rows * SIDE * half, bytes_accessed=2 * tokens.shape[1] * half, transcendentals=0)
    got.append(to_mate(partial_sums(mate_half, [last], cost=cost)))
    own_sums.append(partial_sums(own_half, [last], cost=cost))
    gate_out = combine(place, *own_sums, *got)
    return (new_anchor, new_momentum, merged[None], gate_out[None])


def solution(mesh):
    split = jax.sharding.Mesh(mesh.devices.reshape(SIDE, SIDE * SIDE, 2), ("replica", "chip", "core"))
    fsdp = ("chip", "core")
    return jax.shard_map(
        on_device,
        mesh=split,
        in_specs=(
            P(fsdp, None),
            P(fsdp, None),
            P("replica", fsdp, None),
            P("replica", fsdp, None),
        ),
        out_specs=(
            P(fsdp, None),
            P(fsdp, None),
            P("replica", fsdp, None),
            P("replica", fsdp, None),
        ),
        check_vma=False,
    )
```

```python
import functools

import jax
import jax.numpy as jnp
from jax import lax
from jax.experimental import pallas as pl
from jax.experimental.pallas import tpu as pltpu
from jax.sharding import PartitionSpec as P

SIDE = 4
BLOCK = 128
CHUNKS = 2
MERGE_COLS = 512
UPDATE_COLS = 2048
CHEAP = pl.CostEstimate(flops=1024, bytes_accessed=1024, transcendentals=0)
MIB = 1024 * 1024


def fsdp_index(y, x, core):
    return ((y % SIDE) * SIDE + x % SIDE) * 2 + core


def ring_pairs(step, second):
    pairs = []
    for y in range(SIDE):
        for x in range(SIDE):
            for core in range(2):
                along_x = (core == 0) != second
                target = (y, x + step) if along_x else (y + step, x)
                pairs.append((fsdp_index(y, x, core), fsdp_index(*target, core)))
    return pairs


def in_hbm(value):
    return pltpu.with_memory_space_constraint(value, pltpu.HBM)


def in_vmem(value):
    return pltpu.with_memory_space_constraint(value, pltpu.VMEM)


def to_mate(value):
    return lax.ppermute(value, "core", [(0, 1), (1, 0)])


def to_ring(value, step, second):
    return lax.ppermute(value, ("chip", "core"), ring_pairs(step, second))


def to_replica(value, step):
    return lax.ppermute(value, "replica", [(i, (i + step) % SIDE) for i in range(SIDE)])


def merge_body(anchor, momentum, gathered, outer_grad, merged):
    rows, width = anchor.shape
    blocks = MERGE_COLS // BLOCK
    size = blocks * rows
    spread = jnp.full((BLOCK, BLOCK), 4.0 / BLOCK, jnp.bfloat16)

    def stacked(value):
        return jnp.concatenate([value[:, i * BLOCK : (i + 1) * BLOCK] for i in range(blocks)], axis=0)

    for start in range(0, width, MERGE_COLS):
        cols = slice(start, start + MERGE_COLS)
        local = gathered[:, cols].astype(jnp.float32)
        local = jnp.concatenate([stacked(local[r * rows : (r + 1) * rows]) for r in range(SIDE)], axis=0)
        base = stacked(anchor[:, cols])
        delta = jnp.concatenate([base] * SIDE, axis=0) - local
        square = delta * delta
        high = square.astype(jnp.bfloat16)
        low = (square - high.astype(jnp.float32)).astype(jnp.bfloat16)
        mean = jnp.dot(high, spread, preferred_element_type=jnp.float32)
        mean = mean + jnp.dot(low, spread, preferred_element_type=jnp.float32) + 4e-06
        scale = (mean * lax.rsqrt(mean)).astype(jnp.bfloat16).astype(jnp.float32)
        codes = jnp.clip(delta * pl.reciprocal(scale), -1.0, 1.0).astype(jnp.bfloat16)
        decoded = codes.astype(jnp.float32) * scale
        parts = [decoded[r * size : (r + 1) * size] for r in range(SIDE)]
        grad = ((parts[0] + parts[2]) + (parts[1] + parts[3])) * 0.25
        speed = 0.9 * stacked(momentum[:, cols]) + grad
        anchored = base - 0.7 * (grad + 0.9 * speed)
        blend = (0.5 * local + 0.5 * jnp.concatenate([anchored] * SIDE, axis=0)).astype(merged.dtype)
        for i in range(blocks):
            place = slice(start + i * BLOCK, start + (i + 1) * BLOCK)
            outer_grad[:, place] = grad[i * rows : (i + 1) * rows]
            for r in range(SIDE):
                merged[r * rows : (r + 1) * rows, place] = blend[r * size + i * rows : r * size + (i + 1) * rows]


def merge(anchor, momentum, gathered):
    vmem = pl.BlockSpec(memory_space=pltpu.VMEM)
    return pl.pallas_call(
        merge_body,
        in_specs=[vmem] * 3,
        out_specs=[vmem] * 2,
        out_shape=[
            jax.ShapeDtypeStruct(anchor.shape, jnp.float32),
            jax.ShapeDtypeStruct(gathered.shape, jnp.bfloat16),
        ],
        compiler_params=pltpu.CompilerParams(vmem_limit_bytes=8 * MIB),
        cost_estimate=CHEAP,
        name="merge",
    )(in_vmem(anchor), in_vmem(momentum), in_vmem(gathered))


def update_body(anchor, momentum, local, outer_grad, new_anchor, new_momentum, merged):
    grad = outer_grad[...]
    speed = 0.9 * momentum[...] + grad
    anchored = anchor[...] - 0.7 * (grad + 0.9 * speed)
    new_momentum[...] = speed
    new_anchor[...] = anchored
    merged[...] = (0.5 * local[...].astype(jnp.float32) + 0.5 * anchored).astype(merged.dtype)


def update(anchor, momentum, local, outer_grad):
    rows, width = anchor.shape
    tile = pl.BlockSpec((rows, UPDATE_COLS), lambda i: (0, i))
    wide = jax.ShapeDtypeStruct((rows, width), jnp.float32)
    return pl.pallas_call(
        update_body,
        grid=(width // (UPDATE_COLS),),
        in_specs=[tile] * 4,
        out_specs=[tile] * 3,
        out_shape=[wide, wide, jax.ShapeDtypeStruct((rows, width), jnp.bfloat16)],
        compiler_params=pltpu.CompilerParams(vmem_limit_bytes=12 * MIB),
        cost_estimate=CHEAP,
        name="update",
    )(in_hbm(anchor), in_hbm(momentum), in_hbm(local), outer_grad)


def load_body(entry, place, tokens, *refs):
    half, sem = refs[-2:]
    start = pl.multiple_of(place[entry], half.shape[1])
    copy = pltpu.make_async_copy(tokens.at[:, pl.ds(start, half.shape[1])], half, sem)
    copy.start()
    copy.wait()


def load_columns(place, entry, tokens, width, *earlier):
    anywhere = pl.BlockSpec(memory_space=pl.ANY)
    return pl.pallas_call(
        functools.partial(load_body, entry),
        in_specs=[pl.BlockSpec(memory_space=pltpu.SMEM), pl.BlockSpec(memory_space=pltpu.HBM)]
        + [anywhere] * len(earlier),
        out_specs=pl.BlockSpec(memory_space=pltpu.VMEM),
        out_shape=pltpu.VMEM((tokens.shape[0], width), tokens.dtype),
        scratch_shapes=[pltpu.SemaphoreType.DMA(())],
        compiler_params=pltpu.CompilerParams(vmem_limit_bytes=9 * MIB),
        cost_estimate=CHEAP,
        name="load_columns",
    )(place, in_hbm(tokens), *earlier)


def partial_body(per_block, first, count, tokens, *refs):
    weights, out = refs[: count * per_block], refs[-1]
    for block in range(count):
        start, total = 0, None
        for piece in weights[block * per_block : (block + 1) * per_block]:
            term = lax.dot_general(
                tokens[:, start : start + piece.shape[1]],
                piece[...],
                (((1,), (1,)), ((), ())),
                preferred_element_type=jnp.float32,
            )
            total = term if total is None else total + term
            start += piece.shape[1]
        out[first + block] = total.astype(out.dtype)


def partial_sums(tokens, weights, size=None, filled=None, earlier=(), cost=CHEAP):
    count, half = tokens.shape
    blocks, per_block = len(weights), len(weights[0])
    units = weights[0][0].shape[0]
    size = size or blocks
    vmem = pl.BlockSpec(memory_space=pltpu.VMEM)
    anywhere = pl.BlockSpec(memory_space=pl.ANY)
    more = list(earlier) if filled is None else [*earlier, filled]
    operands = 1 + blocks * per_block
    return pl.pallas_call(
        functools.partial(partial_body, per_block, 0 if filled is None else size - blocks, blocks),
        in_specs=[vmem] * operands + [anywhere] * len(earlier) + ([] if filled is None else [vmem]),
        out_specs=vmem,
        out_shape=jax.ShapeDtypeStruct((size, count, units), jnp.bfloat16),
        input_output_aliases={} if filled is None else {operands + len(earlier): 0},
        compiler_params=pltpu.CompilerParams(vmem_limit_bytes=12 * MIB),
        cost_estimate=cost,
        name="partial_sums",
    )(in_vmem(tokens), *[in_vmem(piece) for block in weights for piece in block], *more)


COMBINE_ROWS = 128


def combine_body(place, own_first, own_mid, own_last, got_first, got_mid, got_last, out, held):
    core = place[0]
    for side, base, first, mid, last in (
        (core, place[1], own_first, own_mid, own_last),
        (1 - core, place[2], got_first, got_mid, got_last),
    ):
        for step, source in ((0, first[0]), (1, mid[0]), (3, mid[1]), (2, last[0])):
            held[side, lax.rem(base + step, SIDE)] = source
    low = lax.broadcasted_iota(jnp.int32, (COMBINE_ROWS, BLOCK), 1) < BLOCK // 2
    for x in (0, 2):
        for k in range(SIDE // 2):
            cols = slice(k * BLOCK, (k + 1) * BLOCK)
            left = held[1, x, :, cols].astype(jnp.float32)
            right = held[1, x + 1, :, cols].astype(jnp.float32)
            crossed = pltpu.roll(jnp.where(low, right, left), BLOCK // 2, 1)
            for y, term in ((2 * k, jnp.where(low, left, crossed)), (2 * k + 1, jnp.where(low, crossed, right))):
                natural = held[0, y, :, slice(x // 2 * BLOCK, (x // 2 + 1) * BLOCK)].astype(jnp.float32)
                start = (2 * y + x // 2) * BLOCK
                out[:, start : start + BLOCK] = (natural + term).astype(out.dtype)


def combine(place, *sums):
    _, count, units = sums[0].shape
    return pl.pallas_call(
        combine_body,
        grid=(count // COMBINE_ROWS,),
        in_specs=[pl.BlockSpec(memory_space=pltpu.SMEM)] + [pl.BlockSpec((value.shape[0], COMBINE_ROWS, units), lambda i: (0, i, 0)) for value in sums],
        out_specs=pl.BlockSpec((COMBINE_ROWS, units * SIDE), lambda i: (i, 0)),
        out_shape=jax.ShapeDtypeStruct((count, units * SIDE), jnp.bfloat16),
        scratch_shapes=[pltpu.VMEM((2, SIDE, COMBINE_ROWS, units), jnp.bfloat16)],
        compiler_params=pltpu.CompilerParams(vmem_limit_bytes=6 * MIB),
        cost_estimate=CHEAP,
        name="combine",
    )(place, *sums)


def follow_body(*refs):
    pass


def follow(values, *earlier):
    vmem = pl.BlockSpec(memory_space=pltpu.VMEM)
    anywhere = pl.BlockSpec(memory_space=pl.ANY)
    return pl.pallas_call(
        follow_body,
        in_specs=[vmem] * len(values) + [anywhere] * len(earlier),
        out_specs=[vmem] * len(values),
        out_shape=[pltpu.VMEM(value.shape, value.dtype) for value in values],
        input_output_aliases={i: i for i in range(len(values))},
        compiler_params=pltpu.CompilerParams(vmem_limit_bytes=4 * MIB),
        cost_estimate=CHEAP,
        name="follow",
    )(*[in_vmem(value) for value in values], *earlier)


def on_device(anchor, momentum, local_weights, tokens):
    rows, width = anchor.shape
    half = width // 2
    part = half // CHUNKS
    replica = lax.axis_index("replica")
    core = lax.axis_index("core")
    chip = lax.axis_index("chip")
    x = chip % SIDE
    y = chip // SIDE
    first_base = jnp.where(core == 0, x, y)
    second_base = jnp.where(core == 0, y, x)
    local = local_weights[0]
    batch = tokens[0]

    share = rows // SIDE
    mine, other = core * half, (1 - core) * half
    row = replica * share
    place = jnp.stack([core, second_base, first_base, mine, other]).astype(jnp.int32)

    def both_cores(own, got):
        return jnp.where(core == 0, jnp.stack([own, got]), jnp.stack([got, own]))

    def columns(value, start):
        return lax.dynamic_slice(value, (0, start), (value.shape[0], half))

    state = jnp.concatenate(
        [lax.dynamic_slice(value, (row, 0), (share, width)) for value in (anchor, momentum)], axis=0
    )
    local_pair = both_cores(columns(local, mine), to_mate(columns(local, other)))
    state_pair = both_cores(columns(state, mine), to_mate(columns(state, other)))
    local_pair = local_pair.reshape(2, SIDE, share, half).transpose(1, 0, 2, 3)
    own_anchor, own_momentum = state_pair.reshape(2, 2, share, half).transpose(1, 0, 2, 3).reshape(2, 2 * share, half)

    def share_of(value, step):
        return lax.dynamic_slice(value, ((replica + step) % SIDE, 0, 0, 0), (1,) + value.shape[1:])

    def exchange(value):
        pieces = [(step, to_replica(share_of(value, step), step)) for step in (1, 3, 2)]
        return [(0, share_of(value, 0))] + pieces

    gathered = jnp.zeros_like(local_pair)
    received = exchange(local_pair)
    mate_half = to_mate(load_columns(place, 4, batch, half, received[1][1], own_anchor))
    for step, piece in received:
        gathered = lax.dynamic_update_slice(gathered, piece, ((replica - step) % SIDE, 0, 0, 0))
    gathered = gathered.reshape(SIDE * 2 * share, half)
    outer_part, merged_parts = merge(own_anchor, own_momentum, gathered)
    outer_part = outer_part.reshape(2, share, half)
    own_part, mate_part = (lax.dynamic_slice(outer_part, (which, 0, 0), (1, share, half))[0] for which in (core, 1 - core))
    mate_part = to_mate(mate_part)
    outer_part = jnp.where(
        core == 0, jnp.concatenate([own_part, mate_part], axis=1), jnp.concatenate([mate_part, own_part], axis=1)
    )
    pair = jnp.zeros((2, SIDE, share, half), jnp.bfloat16)
    for step, piece in exchange(merged_parts.reshape(SIDE, 2, share, half)):
        pair = lax.dynamic_update_slice(pair, piece.reshape(2, 1, share, half), (0, (replica - step) % SIDE, 0, 0))
    pair = pair.reshape(2 * rows, half)

    own_half = load_columns(place, 3, batch, half, pair)
    block = jnp.zeros((SIDE, 2 * rows, half), jnp.bfloat16)
    pieces = [pair] + [to_ring(pair, step, False) for step in (1, 3, 2)]
    for step, piece in zip((0, 1, 3, 2), pieces):
        block = lax.dynamic_update_slice(block, piece[None], ((first_base - step) % SIDE, 0, 0))
    whole = block.reshape(SIDE * 2 * rows, half)
    blocks = []
    for c in range(CHUNKS):
        block = whole[:, c * part : (c + 1) * part]
        blocks.append((block, to_ring(block, SIDE - 1, True), to_ring(block, 1, True)))

    outer_grad = jnp.zeros((rows, width), jnp.float32)
    outer_grad = lax.dynamic_update_slice(outer_grad, outer_part, (row, 0))
    neighbour = lax.ppermute(outer_part, "replica", [(i, i ^ 1) for i in range(SIDE)])
    outer_grad = lax.dynamic_update_slice(outer_grad, neighbour, ((replica ^ 1) * share, 0))
    both = jnp.concatenate([outer_part, neighbour])
    opposite = lax.ppermute(both, "replica", [(i, i ^ 3) for i in range(SIDE)])
    outer_grad = lax.dynamic_update_slice(outer_grad, opposite[:share], ((replica ^ 3) * share, 0))
    outer_grad = lax.dynamic_update_slice(outer_grad, opposite[share:], ((replica ^ 2) * share, 0))
    new_anchor, new_momentum, merged = update(anchor, momentum, local, outer_grad)
    first = [[b[0] for b in blocks]]
    middle = [[b[1] for b in blocks], [b[2] for b in blocks]]
    sums = [partial_sums(mate_half, first)]
    own_sums = [partial_sums(own_half, first)]
    last = []
    for c, (_, following, before) in enumerate(blocks):
        low, high = before[:, : part // 2], following[:, part // 2 :]
        if c == 0:
            low, high = follow([low, high], own_sums[0], merged)
        last += [to_ring(low, 1, True), to_ring(high, SIDE - 1, True)]
    sums.append(partial_sums(mate_half, middle))
    own_sums.append(partial_sums(own_half, middle))
    sums = follow(sums, last[2], own_sums[1])
    got = [to_mate(value) for value in sums]
    cost = pl.CostEstimate(flops=2 * tokens.shape[1] * 2 * rows * SIDE * half, bytes_accessed=2 * tokens.shape[1] * half, transcendentals=0)
    got.append(to_mate(partial_sums(mate_half, [last], cost=cost)))
    own_sums.append(partial_sums(own_half, [last], cost=cost))
    gate_out = combine(place, *own_sums, *got)
    return (new_anchor, new_momentum, merged[None], gate_out[None])


def solution(mesh):
    split = jax.sharding.Mesh(mesh.devices.reshape(SIDE, SIDE * SIDE, 2), ("replica", "chip", "core"))
    fsdp = ("chip", "core")
    return jax.shard_map(
        on_device,
        mesh=split,
        in_specs=(
            P(fsdp, None),
            P(fsdp, None),
            P("replica", fsdp, None),
            P("replica", fsdp, None),
        ),
        out_specs=(
            P(fsdp, None),
            P(fsdp, None),
            P("replica", fsdp, None),
            P("replica", fsdp, None),
        ),
        check_vma=False,
    )
```
